256 devices in a mesh: seq: 32 (over x, y, core), grp: 8 (over z).
Axes of the slice: x: 4, y: 4, z: 8, core: 2. Of those that a mesh axis runs over, the one named last changes fastest.
Arguments:
- projected: bfloat16 [3, 8, 4096, 4096], P(None, 'grp', 'seq'), may hold values from -6 to 6
- short_filter: float32 [3, 3, 4096], replicated, may hold values from -3 to 3
- bias: float32 [4096], replicated, may hold values from -4 to 4
- residue: float32 [16, 4096], replicated, may hold values from -0.09375 to 0.09375
- rate: float32 [16, 4096], replicated, may hold values from 0.0001 to 0.05
- out_weight: bfloat16 [4096, 4096], P(None, 'grp'), may hold values from -0.09375 to 0.09375
Outputs:
- mixed: bfloat16 [8, 4096, 4096], P(None, 'seq', 'grp')
The draws below stay inside these ranges and needn't reach their ends.
All inputs are finite; a program needn't handle non-finite values.
Results may differ from the reference program's by a relative error of at most 0.017.
Values may be sent and summed in bfloat16 or wider, within the bound.
A program may use at most 320 MiB of HBM per device.

```python
import math
import jax
import jax.numpy as jnp
from jax import lax

D = 4096
MODES = 16
SHORT = 3
LEN = 4096
SEQS = 8


def block_levels(stream_key, dims, split, smallest, largest):
    level = 1.0
    for axis_at, parts in split:
        steps = jax.random.uniform(jax.random.fold_in(jax.random.fold_in(stream_key, 6), axis_at), (parts,), jnp.float32, smallest / len(split), largest / len(split))
        level = level * jnp.repeat(jnp.exp(steps), dims[axis_at] // parts).reshape((-1,) + (1,) * (len(dims) - 1 - axis_at))
    return level


def bell_draw(own_key, dims, scale, bound, shards=(), held_as=jnp.bfloat16):
    result = scale * jax.random.normal(own_key, dims, jnp.float32)
    if shards:
        result = result * block_levels(own_key, dims, shards, -0.22, 0.18)
    return jnp.clip(result, -bound, bound).astype(held_as)


def setup_inputs(seed: int = 0) -> dict:
    streams_of = jax.random.split(jax.random.key(seed), 7)
    projected = bell_draw(streams_of[0], (3, SEQS, LEN, D), 1.0, 6.0, ((1, 8), (2, 32)))
    short_filter = bell_draw(streams_of[1], (3, SHORT, D), 0.5, 3.0, (), jnp.float32)
    bias = bell_draw(streams_of[2], (D,), 1.0, 4.0, (), jnp.float32)
    residue = bell_draw(streams_of[3], (MODES, D), LEN ** -0.5, 0.09375, (), jnp.float32)
    rate = jnp.clip(jnp.exp(jax.random.uniform(streams_of[4], (MODES, D), jnp.float32, math.log(0.0001), math.log(0.05))), 0.0001, 0.05)
    out_weight = bell_draw(streams_of[5], (D, D), D ** -0.5, 0.09375, ((1, 8),))
    return {"projected": projected, "short_filter": short_filter, "bias": bias, "residue": residue, "rate": rate, "out_weight": out_weight}


def reference(projected, short_filter, bias, residue, rate, out_weight):
    positions = jnp.arange(LEN, dtype=jnp.float32)
    impulse = jnp.zeros((LEN, D), jnp.float32)
    for mode_index in range(MODES):
        impulse = impulse + residue[mode_index][None, :] * jnp.exp(-rate[mode_index][None, :] * positions[:, None])
    impulse_freq = jnp.fft.rfft(impulse, n=2 * LEN, axis=0)

    def one_sequence(stacked):
        extended = jnp.pad(stacked.astype(jnp.float32), ((0, 0), (SHORT - 1, 0), (0, 0)))
        featured = short_filter[:, 0][:, None, :] * extended[:, SHORT - 1:, :]
        for offset in range(1, SHORT):
            featured = featured + short_filter[:, offset][:, None, :] * extended[:, SHORT - 1 - offset:SHORT - 1 - offset + LEN, :]
        product = featured[1] * featured[2]
        joined_freq = jnp.fft.rfft(product, n=2 * LEN, axis=0) * impulse_freq
        convolved = jnp.fft.irfft(joined_freq, n=2 * LEN, axis=0)[:LEN]
        return (featured[0] * (convolved + bias[None, :] * product)).astype(jnp.bfloat16)

    gated = lax.map(one_sequence, jnp.moveaxis(projected, 1, 0))
    flat_rows = gated.reshape(SEQS * LEN, D)
    mixed = jnp.dot(flat_rows, out_weight, preferred_element_type=jnp.float32).astype(jnp.bfloat16)
    return mixed.reshape(SEQS, LEN, D)
```

```python
import functools

import jax
import jax.numpy as jnp
from jax import lax
from jax.experimental import pallas as pl
from jax.experimental.pallas import tpu as pltpu
from jax.sharding import PartitionSpec as P

LANES = 128
GROUPS = 8
MIB = 1024 * 1024


def wide(row):
    return jnp.broadcast_to(row, (GROUPS, LANES))


def first_pass(lanes, steps, modes, halo, projected, taps, rate, extended, queries, product, starts, ends):
    count = steps * GROUPS
    for c in range(3):
        extended[c, pl.ds(0, 8), :] = halo[c, :, lanes].astype(jnp.float32)
        extended[c, pl.ds(8, count), :] = projected[c, :, lanes].astype(jnp.float32)
    decay = [wide(jnp.exp(-rate[pl.ds(m, 1), lanes])) for m in range(modes)]
    tap = [[wide(taps[c, pl.ds(j, 1), lanes]) for j in range(3)] for c in range(3)]
    state = [None] * modes
    held = [[extended[c, pl.ds(8 - j, GROUPS, stride=steps), :] for j in (2, 1)] for c in range(3)]
    for i in range(steps):
        featured = []
        for c in range(3):
            now = extended[c, pl.ds(8 + i, GROUPS, stride=steps), :]
            featured.append(tap[c][0] * now + tap[c][1] * held[c][1] + tap[c][2] * held[c][0])
            held[c] = [held[c][1], now]
        x = featured[1] * featured[2]
        queries[i, :, lanes] = featured[0]
        product[i, :, lanes] = x
        for m in range(modes):
            state[m] = x if i == 0 else decay[m] * state[m] + x
    row = lax.broadcasted_iota(jnp.int32, (GROUPS, LANES), 0)
    for m in range(modes):
        here = state[m]
        speed = wide(rate[pl.ds(m, 1), lanes])
        for distance in (1, 2, 4):
            factor = jnp.where(row >= distance, jnp.exp(speed * (-float(steps * distance))), 0.0)
            here = here + factor * pltpu.roll(here, distance, 0)
        starts[m, :, lanes] = jnp.where(row >= 1, pltpu.roll(here, 1, 0), 0.0)
        ends[pl.ds(m, 1), lanes] = here[GROUPS - 1 :, :]


def second_pass(lanes, steps, modes, queries, product, starts, before, rate, residue, bias, ordered, gated):
    row = lax.broadcasted_iota(jnp.int32, (GROUPS, LANES), 0).astype(jnp.float32)
    decay, weight, state = [], [], []
    for m in range(modes):
        speed = wide(rate[pl.ds(m, 1), lanes])
        decay.append(jnp.exp(-speed))
        weight.append(wide(residue[pl.ds(m, 1), lanes]))
        carried = jnp.exp(speed * row * (-float(steps))) * wide(before[pl.ds(m, 1), lanes])
        state.append(starts[m, :, lanes] + carried)
    skip = wide(bias[pl.ds(0, 1), lanes])
    for i in range(steps):
        x = product[i, :, lanes]
        total = skip * x
        for m in range(modes):
            state[m] = decay[m] * state[m] + x
            total = total + weight[m] * state[m]
        ordered[pl.ds(i, GROUPS, stride=steps), :] = queries[i, :, lanes] * total
    gated[:, lanes] = ordered[...].astype(jnp.bfloat16)


def first_kernel(steps, modes, halo, projected, taps, rate, queries, product, starts, ends, extended):
    @pl.loop(0, projected.shape[-1] // LANES)
    def _(slab):
        lanes = pl.ds(pl.multiple_of(slab * LANES, LANES), LANES)
        first_pass(lanes, steps, modes, halo, projected, taps, rate, extended, queries, product, starts, ends)


def scan_kernel(rate, ends, before):
    factor = jnp.exp(-float(SPAN) * rate[...])
    carried = jnp.zeros_like(factor)
    for r in range(ends.shape[0]):
        before[r] = carried
        carried = factor * carried + ends[r]


SPAN = 128


def second_kernel(steps, modes, queries, product, starts, before, rate, residue, bias, gated, ordered):
    @pl.loop(0, gated.shape[-1] // LANES)
    def _(slab):
        lanes = pl.ds(pl.multiple_of(slab * LANES, LANES), LANES)
        second_pass(lanes, steps, modes, queries, product, starts, before, rate, residue, bias, ordered, gated)


def on_device(projected, short_filter, bias, residue, rate, out_weight):
    ranks = lax.axis_size("seq")
    rank = lax.axis_index("seq")
    taken = projected[:, 0]
    rows, width = taken.shape[1:]
    modes = rate.shape[0]
    steps = rows // GROUPS
    edge = taken[:, rows - 8 :, :]
    halo = lax.ppermute(edge, "seq", [(i, i + 1) for i in range(ranks - 1)])
    f32 = jnp.float32
    params = pltpu.CompilerParams(vmem_limit_bytes=40 * MIB)
    vmem = pl.BlockSpec(memory_space=pltpu.VMEM)
    block = lambda *lead: pl.BlockSpec(lead + (512,), lambda k: (0,) * len(lead) + (k,))
    queries, product, starts, ends = pl.pallas_call(
        functools.partial(first_kernel, steps, modes),
        grid=(width // 512,),
        in_specs=[block(3, 8), block(3, rows), block(3, 3), block(modes)],
        out_specs=[block(steps, GROUPS), block(steps, GROUPS), block(modes, GROUPS), block(modes)],
        out_shape=[
            jax.ShapeDtypeStruct((steps, GROUPS, width), f32),
            jax.ShapeDtypeStruct((steps, GROUPS, width), f32),
            jax.ShapeDtypeStruct((modes, GROUPS, width), f32),
            jax.ShapeDtypeStruct((modes, width), f32),
        ],
        scratch_shapes=[pltpu.VMEM((3, rows + 8, LANES), f32)],
        compiler_params=params,
    )(halo, taken, short_filter, rate)
    part = width // ranks
    spread = lax.all_to_all(
        jnp.moveaxis(ends.reshape(modes, ranks, part), 1, 0), "seq", split_axis=0, concat_axis=0, tiled=True
    )
    own = lax.dynamic_slice_in_dim(rate, rank * part, part, axis=1)
    before = pl.pallas_call(
        scan_kernel,
        in_specs=[vmem, vmem],
        out_specs=vmem,
        out_shape=jax.ShapeDtypeStruct((ranks, modes, part), f32),
        compiler_params=params,
    )(own, spread)
    before = lax.all_to_all(before, "seq", split_axis=0, concat_axis=0, tiled=True)
    before = jnp.moveaxis(before, 0, 1).reshape(modes, width)
    gated = pl.pallas_call(
        functools.partial(second_kernel, steps, modes),
        grid=(width // 512,),
        in_specs=[
            block(steps, GROUPS),
            block(steps, GROUPS),
            block(modes, GROUPS),
            block(modes),
            block(modes),
            block(modes),
            block(1),
        ],
        out_specs=block(rows),
        out_shape=jax.ShapeDtypeStruct((rows, width), jnp.bfloat16),
        scratch_shapes=[pltpu.VMEM((rows, LANES), f32)],
        compiler_params=params,
    )(queries, product, starts, before, rate, residue, bias[None])
    return jnp.einsum(
        "srd,de->sre",
        lax.all_gather(gated[None], "grp", axis=0, tiled=True),
        out_weight,
        preferred_element_type=jnp.float32,
    ).astype(jnp.bfloat16)


def solution(mesh):
    placed = (P(None, "grp", "seq", None), P(), P(), P(), P(), P(None, "grp"))
    return jax.shard_map(
        on_device, mesh=mesh, in_specs=placed, out_specs=P(None, "seq", "grp"), check_vma=False
    )
```

```python
import functools

import jax
import jax.numpy as jnp
from jax import lax
from jax.experimental import pallas as pl
from jax.experimental.pallas import tpu as pltpu
from jax.sharding import PartitionSpec as P

LANES = 128
GROUPS = 8
MIB = 1024 * 1024


MESH = pl.DeviceIdType.MESH


def slab_lanes(slab):
    return pl.ds(pl.multiple_of(slab * LANES, LANES), LANES)


def wide(row):
    return jnp.broadcast_to(row, (GROUPS, LANES))


def first_pass(slab, keep, steps, modes, halo, projected, taps, rate, extended, queries, product, starts, ends):
    lanes = slab_lanes(slab)
    count = steps * GROUPS
    for c in range(3):
        extended[c, pl.ds(6, 2), :] = halo[pl.ds(2 * c, 2), lanes] * keep
        extended[c, pl.ds(8, count), :] = projected[c, :, lanes].astype(jnp.float32)
    decay = [wide(jnp.exp(-rate[pl.ds(m, 1), lanes])) for m in range(modes)]
    tap = [[wide(taps[c, pl.ds(j, 1), lanes]) for j in range(3)] for c in range(3)]
    state = [None] * modes
    held = [[extended[c, pl.ds(8 - j, GROUPS, stride=steps), :] for j in (2, 1)] for c in range(3)]
    for i in range(steps):
        featured = []
        for c in range(3):
            now = extended[c, pl.ds(8 + i, GROUPS, stride=steps), :]
            featured.append(tap[c][0] * now + tap[c][1] * held[c][1] + tap[c][2] * held[c][0])
            held[c] = [held[c][1], now]
        x = featured[1] * featured[2]
        queries[i, :, lanes] = featured[0]
        product[i, :, lanes] = x
        for m in range(modes):
            state[m] = x if i == 0 else decay[m] * state[m] + x
    row = lax.broadcasted_iota(jnp.int32, (GROUPS, LANES), 0)
    for m in range(modes):
        here = state[m]
        speed = wide(rate[pl.ds(m, 1), lanes])
        for distance in (1, 2, 4):
            factor = jnp.where(row >= distance, jnp.exp(speed * (-float(steps * distance))), 0.0)
            here = here + factor * pltpu.roll(here, distance, 0)
        starts[m, :, lanes] = jnp.where(row >= 1, pltpu.roll(here, 1, 0), 0.0)
        ends[slab, pl.ds(m, 1), :] = here[GROUPS - 1 :, :]


def second_pass(slab, steps, modes, queries, product, starts, before, rate, residue, bias, ordered):
    lanes = slab_lanes(slab)
    row = lax.broadcasted_iota(jnp.int32, (GROUPS, LANES), 0).astype(jnp.float32)
    decay, weight, state = [], [], []
    for m in range(modes):
        speed = wide(rate[pl.ds(m, 1), lanes])
        decay.append(jnp.exp(-speed))
        weight.append(wide(residue[pl.ds(m, 1), lanes]))
        carried = jnp.exp(speed * row * (-float(steps))) * wide(before[slab, pl.ds(m, 1), :])
        state.append(starts[m, :, lanes] + carried)
    skip = wide(bias[pl.ds(0, 1), lanes])
    for i in range(steps):
        x = product[i, :, lanes]
        total = skip * x
        for m in range(modes):
            state[m] = decay[m] * state[m] + x
            total = total + weight[m] * state[m]
        ordered[pl.ds(i, GROUPS, stride=steps), :] = queries[i, :, lanes] * total
    return ordered[...].astype(jnp.bfloat16)


def front_kernel(
    ranks,
    steps,
    modes,
    projected,
    taps,
    rate,
    residue,
    bias,
    gated,
    extended,
    ordered,
    queries,
    product,
    starts,
    edge,
    halo,
    ends,
    spread,
    back,
    before,
    edge_sem,
    ends_sem,
    back_sem,
):
    rank = lax.axis_index("seq")
    column = lax.axis_index("grp")
    rows = steps * GROUPS

    barrier = pltpu.get_barrier_semaphore()

    @pl.loop(1, ranks)
    def _(i):
        pl.semaphore_signal(
            barrier, inc=1, device_id=(lax.rem(rank + i, ranks), column), device_id_type=MESH
        )

    for c in range(3):
        edge[pl.ds(2 * c, 2), :] = projected[c, pl.ds(rows - 16, 16), :].astype(jnp.float32)[14:, :]
    pl.semaphore_wait(barrier, ranks - 1)

    edge_copy = pltpu.make_async_remote_copy(
        src_ref=edge,
        dst_ref=halo,
        send_sem=edge_sem.at[0],
        recv_sem=edge_sem.at[1],
        device_id=(lax.rem(rank + 1, ranks), column),
        device_id_type=MESH,
    )
    edge_copy.start()
    edge_copy.wait_recv()
    keep = jnp.where(rank > 0, 1.0, 0.0)

    def ends_copy(owner):
        return pltpu.make_async_remote_copy(
            src_ref=ends.at[owner],
            dst_ref=spread.at[rank],
            send_sem=ends_sem.at[0],
            recv_sem=ends_sem.at[1],
            device_id=(owner, column),
            device_id_type=MESH,
        )

    @pl.loop(0, ranks)
    def _(slab):
        first_pass(slab, keep, steps, modes, halo, projected, taps, rate, extended, queries, product, starts, ends)

        @pl.when(slab == rank)
        def _():
            spread[rank] = ends[rank]

        @pl.when(slab != rank)
        def _():
            ends_copy(slab).start()

    def all_but_one(ref, send_sem, recv_sem):
        return pltpu.make_async_remote_copy(
            src_ref=ref.at[pl.ds(0, ranks - 1)],
            dst_ref=ref.at[pl.ds(0, ranks - 1)],
            send_sem=send_sem,
            recv_sem=recv_sem,
            device_id=(lax.rem(rank + 1, ranks), column),
            device_id_type=MESH,
        )

    all_but_one(spread, ends_sem.at[0], ends_sem.at[1]).wait_recv()
    factor = jnp.exp(rate[:, slab_lanes(rank)] * (-float(rows)))
    carried = jnp.zeros_like(factor)
    for r in range(ranks):
        back[r] = carried
        carried = factor * carried + spread[r]
    before[rank] = back[rank]

    @pl.loop(1, ranks)
    def _(i):
        other = lax.rem(rank + i, ranks)
        pltpu.make_async_remote_copy(
            src_ref=back.at[other],
            dst_ref=before.at[rank],
            send_sem=back_sem.at[0],
            recv_sem=back_sem.at[1],
            device_id=(other, column),
            device_id_type=MESH,
        ).start()

    all_but_one(before, back_sem.at[0], back_sem.at[1]).wait_recv()

    @pl.loop(0, ranks)
    def _(slab):
        gated[:, slab_lanes(slab)] = second_pass(
            slab, steps, modes, queries, product, starts, before, rate, residue, bias, ordered
        )

    edge_copy.wait_send()
    all_but_one(ends, ends_sem.at[0], ends_sem.at[1]).wait_send()
    all_but_one(back, back_sem.at[0], back_sem.at[1]).wait_send()


def on_device(projected, short_filter, bias, residue, rate, out_weight):
    ranks = lax.axis_size("seq")
    taken = projected[:, 0]
    rows, width = taken.shape[1:]
    modes = rate.shape[0]
    steps = rows // GROUPS
    f32 = jnp.float32
    vmem = pl.BlockSpec(memory_space=pltpu.VMEM)
    exchanged = pltpu.VMEM((ranks, modes, width // ranks), f32)
    gated = pl.pallas_call(
        functools.partial(front_kernel, ranks, steps, modes),
        in_specs=[vmem] * 5,
        out_specs=vmem,
        out_shape=jax.ShapeDtypeStruct((rows, width), jnp.bfloat16),
        scratch_shapes=[
            pltpu.VMEM((3, rows + 8, LANES), f32),
            pltpu.VMEM((rows, LANES), f32),
            pltpu.VMEM((steps, GROUPS, width), f32),
            pltpu.VMEM((steps, GROUPS, width), f32),
            pltpu.VMEM((modes, GROUPS, width), f32),
            pltpu.VMEM((8, width), f32),
            pltpu.VMEM((8, width), f32),
            exchanged,
            exchanged,
            exchanged,
            exchanged,
            pltpu.SemaphoreType.DMA((2,)),
            pltpu.SemaphoreType.DMA((2,)),
            pltpu.SemaphoreType.DMA((2,)),
        ],
        compiler_params=pltpu.CompilerParams(
            collective_id=0, has_side_effects=True, vmem_limit_bytes=48 * MIB
        ),
    )(taken, short_filter, rate, residue, bias[None])
    return jnp.einsum(
        "srd,de->sre",
        lax.all_gather(gated[None], "grp", axis=0, tiled=True),
        out_weight,
        preferred_element_type=jnp.float32,
    ).astype(jnp.bfloat16)


def solution(mesh):
    placed = (P(None, "grp", "seq", None), P(), P(), P(), P(), P(None, "grp"))
    return jax.shard_map(
        on_device, mesh=mesh, in_specs=placed, out_specs=P(None, "seq", "grp"), check_vma=False
    )
```

```python
import functools

import jax
import jax.numpy as jnp
from jax import lax
from jax.experimental import pallas as pl
from jax.experimental.pallas import tpu as pltpu
from jax.sharding import PartitionSpec as P

LANES = 128
GROUPS = 8
MIB = 1024 * 1024


MESH = pl.DeviceIdType.MESH


def slab_lanes(slab):
    return pl.ds(pl.multiple_of(slab * LANES, LANES), LANES)


def wide(row):
    return jnp.broadcast_to(row, (GROUPS, LANES))


def first_pass(slab, keep, steps, modes, halo, projected, taps, rate, extended, queries, product, starts, ends):
    lanes = slab_lanes(slab)
    count = steps * GROUPS
    for c in range(3):
        extended[c, pl.ds(6, 2), :] = halo[pl.ds(2 * c, 2), lanes] * keep
        extended[c, pl.ds(8, count), :] = projected[c, :, lanes].astype(jnp.float32)
    decay = [wide(jnp.exp(-rate[pl.ds(m, 1), lanes])) for m in range(modes)]
    tap = [[wide(taps[c, pl.ds(j, 1), lanes]) for j in range(3)] for c in range(3)]
    state = [None] * modes
    held = [[extended[c, pl.ds(8 - j, GROUPS, stride=steps), :] for j in (2, 1)] for c in range(3)]
    for i in range(steps):
        featured = []
        for c in range(3):
            now = extended[c, pl.ds(8 + i, GROUPS, stride=steps), :]
            featured.append(tap[c][0] * now + tap[c][1] * held[c][1] + tap[c][2] * held[c][0])
            held[c] = [held[c][1], now]
        x = featured[1] * featured[2]
        queries[i, :, lanes] = featured[0]
        product[i, :, lanes] = x
        for m in range(modes):
            state[m] = x if i == 0 else decay[m] * state[m] + x
    row = lax.broadcasted_iota(jnp.int32, (GROUPS, LANES), 0)
    for m in range(modes):
        here = state[m]
        speed = wide(rate[pl.ds(m, 1), lanes])
        for distance in (1, 2, 4):
            factor = jnp.where(row >= distance, jnp.exp(speed * (-float(steps * distance))), 0.0)
            here = here + factor * pltpu.roll(here, distance, 0)
        starts[m, :, lanes] = jnp.where(row >= 1, pltpu.roll(here, 1, 0), 0.0)
        ends[slab, pl.ds(m, 1), :] = here[GROUPS - 1 :, :]


def second_pass(slab, steps, modes, queries, product, starts, before, rate, residue, bias, ordered):
    lanes = slab_lanes(slab)
    row = lax.broadcasted_iota(jnp.int32, (GROUPS, LANES), 0).astype(jnp.float32)
    decay, weight, state = [], [], []
    for m in range(modes):
        speed = wide(rate[pl.ds(m, 1), lanes])
        decay.append(jnp.exp(-speed))
        weight.append(wide(residue[pl.ds(m, 1), lanes]))
        carried = jnp.exp(speed * row * (-float(steps))) * wide(before[slab, pl.ds(m, 1), :])
        state.append(starts[m, :, lanes] + carried)
    skip = wide(bias[pl.ds(0, 1), lanes])
    for i in range(steps):
        x = product[i, :, lanes]
        total = skip * x
        for m in range(modes):
            state[m] = decay[m] * state[m] + x
            total = total + weight[m] * state[m]
        ordered[pl.ds(i, GROUPS, stride=steps), :] = queries[i, :, lanes] * total
    return ordered[...].astype(jnp.bfloat16)


BLOCKS = 4
PARTS = 4
CHUNKS = 8
SHARED = 96
SKEW = 2
SCOPE = 4


def block_kernel(
    ranks,
    steps,
    modes,
    projected,
    taps,
    rate,
    residue,
    bias,
    out_weight,
    mixed,
    extended,
    ordered,
    queries,
    product,
    starts,
    edge,
    halo,
    ends,
    spread,
    back,
    before,
    weight,
    gathered,
    total,
    leaving,
    returned,
    edge_sem,
    ends_sem,
    back_sem,
    left_sem,
    right_sem,
    swap_sem,
    twin_sem,
    sent_sem,
    rows_sem,
    return_sem,
    mixed_sem,
):
    rank = lax.axis_index("seq")
    z = lax.axis_index("grp")
    depth = mixed.shape[0]
    rows = steps * GROUPS
    x, y, core = rank // 8, (rank // 2) % 4, rank % 2
    side = y % 2
    q = (x + 2 * (y // 2)) % BLOCKS

    def at(px, py, pcore):
        return (px % 4) * 8 + (py % 4) * 2 + pcore

    x_up, x_down = at(x + 1, y, core), at(x + 3, y, core)
    y_out = at(x, y + 3 + 2 * side, core)
    y_pair = at(x, y + 1 - 2 * side, core)
    twin = at(x, y, 1 - core)

    def remote(source, target, send_sem, recv_sem, to_rank, to_z):
        return pltpu.make_async_remote_copy(
            src_ref=source,
            dst_ref=target,
            send_sem=send_sem,
            recv_sem=recv_sem,
            device_id=(to_rank, to_z),
            device_id_type=MESH,
        )

    barrier = pltpu.get_barrier_semaphore()

    @pl.loop(1, ranks)
    def _(i):
        pl.semaphore_signal(barrier, inc=1, device_id=(lax.rem(rank + i, ranks), z), device_id_type=MESH)

    @pl.loop(1, depth)
    def _(i):
        pl.semaphore_signal(barrier, inc=1, device_id=(rank, lax.rem(z + i, depth)), device_id_type=MESH)

    up = (z + depth - q) % BLOCKS
    down = (q + depth - z) % BLOCKS
    from_above = ((z + down + depth - q) % depth) // BLOCKS
    from_below = 1 - from_above
    span = weight.shape[1] // CHUNKS
    half = span // 2
    taken = half - SHARED
    count = PARTS * CHUNKS

    def weight_rows(j, offset, size, block=None):
        start = pl.multiple_of((j % CHUNKS) * span + core * half + offset, 16)
        columns = pl.ds(0, 2 * LANES) if block is None else slab_lanes(block)
        return weight.at[j // CHUNKS, pl.ds(start, size), columns]

    def moving(j, block, send_sem, recv_sem, to_z):
        view = weight_rows(j, side * SHARED, taken, block)
        return remote(view, view, send_sem, recv_sem.at[j], rank, to_z % depth)

    def upward(j, block):
        return moving(j, block, sent_sem.at[0], left_sem, z + 1)

    def downward(j, block):
        return moving(j, block, sent_sem.at[1], right_sem, z + depth - 1)

    def swap(j, block):
        view = weight_rows(j, side * taken, SHARED, block)
        return remote(view, view, sent_sem.at[2], swap_sem.at[j], y_pair, z)

    def weight_step(n):
        j = n - SKEW * down

        @pl.when((j >= 0) & (j < count))
        def _():
            downward(j, from_above).wait_recv()

            @pl.when(down < BLOCKS - 1)
            def _():
                downward(j, from_above).start()

            @pl.when(up == 0)
            def _():
                upward(j, from_above).start()

            swap(j, from_above).start()

        k = n - SKEW * jnp.where(up == 0, BLOCKS, up)

        @pl.when((k >= 0) & (k < count))
        def _():
            upward(k, from_below).wait_recv()

            @pl.when(up > 0)
            def _():
                upward(k, from_below).start()

            swap(k, from_below).start()

        whole = n - SKEW * (BLOCKS + 1)

        @pl.when((whole >= 0) & (whole < count))
        def _():
            other = weight_rows(whole, (1 - side) * taken, SHARED)
            remote(other, other, sent_sem.at[2], swap_sem.at[whole], y_pair, z).wait_recv()
            view = weight_rows(whole, 0, half)
            remote(view, view, sent_sem.at[3], twin_sem.at[whole // CHUNKS], twin, z).start()

    def weight_steps(first, last):
        @pl.loop(first, last)
        def _(n):
            weight_step(n)

    @pl.when(down == 0)
    def _():
        @pl.loop(0, count)
        def _(j):
            start = pl.multiple_of((j % CHUNKS) * span + core * half + side * SHARED, 16)
            pltpu.make_async_copy(
                out_weight.at[pl.ds(start, taken), slab_lanes(j // CHUNKS)],
                weight_rows(j, side * SHARED, taken, from_above),
                right_sem.at[j],
            ).start()

    for c in range(3):
        edge[pl.ds(2 * c, 2), :] = projected[c, pl.ds(rows - 16, 16), :].astype(jnp.float32)[14:, :]
    pl.semaphore_wait(barrier, ranks + depth - 2)

    edge_copy = remote(edge, halo, edge_sem.at[0], edge_sem.at[1], lax.rem(rank + 1, ranks), z)
    edge_copy.start()
    weight_step(0)
    edge_copy.wait_recv()
    keep = jnp.where(rank > 0, 1.0, 0.0)

    groups = ranks // SCOPE

    @pl.loop(0, groups)
    def _(n):
        weight_step(n + 1)

        @pl.loop(0, SCOPE)
        def _(i):
            slab = n * SCOPE + i
            first_pass(
                slab, keep, steps, modes, halo, projected, taps, rate, extended, queries, product, starts, ends
            )

            @pl.when(slab == rank)
            def _():
                spread[rank] = ends[rank]

            @pl.when(slab != rank)
            def _():
                remote(ends.at[slab], spread.at[rank], ends_sem.at[0], ends_sem.at[1], slab, z).start()

    def all_but_one(ref, sem):
        view = ref.at[pl.ds(0, ranks - 1)]
        return remote(view, view, sem.at[0], sem.at[1], lax.rem(rank + 1, ranks), z)

    weight_steps(groups + 1, groups + 3)
    all_but_one(spread, ends_sem).wait_recv()
    factor = jnp.exp(rate[:, slab_lanes(rank)] * (-float(rows)))
    carried = jnp.zeros_like(factor)
    for r in range(ranks):
        back[r] = carried
        carried = factor * carried + spread[r]
    before[rank] = back[rank]

    @pl.loop(1, ranks)
    def _(i):
        other = lax.rem(rank + i, ranks)
        remote(back.at[other], before.at[rank], back_sem.at[0], back_sem.at[1], other, z).start()

    weight_steps(groups + 3, groups + 5)
    all_but_one(before, back_sem).wait_recv()

    def rows_copy(n, slot, to_rank):
        return remote(
            gathered.at[n, 0], gathered.at[n, slot], rows_sem.at[0], rows_sem.at[slot], to_rank, z
        )

    @pl.loop(0, groups)
    def _(n):
        weight_step(n + groups + 5)

        @pl.loop(0, SCOPE)
        def _(i):
            gathered[n, 0, :, slab_lanes(i)] = second_pass(
                n * SCOPE + i, steps, modes, queries, product, starts, before, rate, residue, bias, ordered
            )

        rows_copy(n, 1, x_up).start()
        rows_copy(n, 2, x_down).start()
        rows_copy(n, 3, y_out).start()

    def return_copy(p, i, slot, to_rank):
        return remote(
            leaving.at[p, i], returned.at[p, slot], return_sem.at[0], return_sem.at[slot + PARTS * p], to_rank, z
        )

    def project(p):
        half_part = weight.at[p, pl.ds(0, weight.shape[1] // 2)]
        remote(half_part, half_part, sent_sem.at[3], twin_sem.at[p], twin, z).wait_recv()

        def term(n):
            block = gathered[n].reshape(BLOCKS * rows, SCOPE * LANES)
            start = pl.multiple_of(n * SCOPE * LANES, SCOPE * LANES)
            return jnp.dot(
                block, weight[p, pl.ds(start, SCOPE * LANES), :], preferred_element_type=jnp.float32
            )

        total[...] = term(0)

        @pl.loop(1, groups)
        def _(n):
            total[...] += term(n)

        for i in range(3):
            leaving[p, i] = total[pl.ds((i + 1) * rows, rows), :].astype(jnp.bfloat16)
        returned[p, 0] = total[pl.ds(0, rows), :].astype(jnp.bfloat16)
        return_copy(p, 0, 2, x_down).start()
        return_copy(p, 1, 1, x_up).start()
        return_copy(p, 2, 3, y_out).start()

    def deliver(p):
        return_copy(p, 0, 2, x_down).wait_recv()
        return_copy(p, 1, 1, x_up).wait_recv()
        return_copy(p, 2, 3, y_out).wait_recv()
        for slot, block in ((0, q), (1, q + 3), (2, q + 1), (3, q + 2)):
            for upper in range(2):
                owner = (block % BLOCKS + BLOCKS * upper) % depth
                view = returned.at[p, slot, :, pl.ds(upper * LANES, LANES)]
                target = mixed.at[z, :, pl.ds(p * LANES, LANES)]

                @pl.when(owner == z)
                def _():
                    target[...] = view[...]

                @pl.when(owner != z)
                def _():
                    remote(view, target, mixed_sem.at[0], mixed_sem.at[1], rank, owner).start()

    weight_steps(2 * groups + 5, count + SKEW * (BLOCKS + 1))
    for slot in (1, 2, 3):
        view = gathered.at[:, slot]
        remote(view, view, rows_sem.at[0], rows_sem.at[slot], x_up, z).wait_recv()
    project(0)
    for p in range(1, PARTS):
        project(p)
        deliver(p - 1)
    deliver(PARTS - 1)

    edge_copy.wait_send()
    all_but_one(ends, ends_sem).wait_send()
    all_but_one(back, back_sem).wait_send()

    def sent(view, sem):
        remote(view, view, sem, left_sem.at[0], x_up, z).wait_send()

    chain = weight.at[0, pl.ds(0, count * taken // 2)]
    sent(chain, sent_sem.at[0])

    @pl.when(down < BLOCKS - 1)
    def _():
        sent(chain, sent_sem.at[1])

    sent(weight.at[0, pl.ds(0, count * SHARED)], sent_sem.at[2])
    sent(weight.at[pl.ds(0, PARTS // 2)], sent_sem.at[3])
    sent(gathered.at[:, pl.ds(0, 3)], rows_sem.at[0])
    sent(leaving, return_sem.at[0])
    others = mixed.at[pl.ds(0, depth - 1)]
    remote(others, others, mixed_sem.at[0], mixed_sem.at[1], x_up, z).wait()


def on_device(projected, short_filter, bias, residue, rate, out_weight):
    ranks = lax.axis_size("seq")
    depth = lax.axis_size("grp")
    taken = projected[:, 0]
    rows, width = taken.shape[1:]
    modes = rate.shape[0]
    steps = rows // GROUPS
    f32, bf16 = jnp.float32, jnp.bfloat16
    vmem = pl.BlockSpec(memory_space=pltpu.VMEM)
    exchanged = pltpu.VMEM((ranks, modes, width // ranks), f32)
    dma = pltpu.SemaphoreType.DMA
    return pl.pallas_call(
        functools.partial(block_kernel, ranks, steps, modes),
        in_specs=[vmem] * 5 + [pl.BlockSpec(memory_space=pl.ANY)],
        out_specs=vmem,
        out_shape=jax.ShapeDtypeStruct((depth, rows, out_weight.shape[1]), bf16),
        scratch_shapes=[
            pltpu.VMEM((3, rows + 8, LANES), f32),
            pltpu.VMEM((rows, LANES), f32),
            pltpu.VMEM((steps, GROUPS, width), f32),
            pltpu.VMEM((steps, GROUPS, width), f32),
            pltpu.VMEM((modes, GROUPS, width), f32),
            pltpu.VMEM((8, width), f32),
            pltpu.VMEM((8, width), f32),
            exchanged,
            exchanged,
            exchanged,
            exchanged,
            pltpu.VMEM((PARTS, width, 2 * LANES), bf16),
            pltpu.VMEM((ranks // SCOPE, BLOCKS, rows, SCOPE * LANES), bf16),
            pltpu.VMEM((BLOCKS * rows, 2 * LANES), f32),
            pltpu.VMEM((PARTS, 3, rows, 2 * LANES), bf16),
            pltpu.VMEM((PARTS, BLOCKS, rows, 2 * LANES), bf16),
            dma((2,)),
            dma((2,)),
            dma((2,)),
            dma((PARTS * CHUNKS,)),
            dma((PARTS * CHUNKS,)),
            dma((PARTS * CHUNKS,)),
            dma((PARTS,)),
            dma((4,)),
            dma((4,)),
            dma((4 * PARTS,)),
            dma((2,)),
        ],
        compiler_params=pltpu.CompilerParams(
            collective_id=0, has_side_effects=True, vmem_limit_bytes=48 * MIB
        ),
    )(taken, short_filter, rate, residue, bias[None], out_weight)


def solution(mesh):
    placed = (P(None, "grp", "seq", None), P(), P(), P(), P(), P(None, "grp"))
    return jax.shard_map(
        on_device, mesh=mesh, in_specs=placed, out_specs=P(None, "seq", "grp"), check_vma=False
    )
```

```python
import functools

import jax
import jax.numpy as jnp
from jax import lax
from jax.experimental import pallas as pl
from jax.experimental.pallas import tpu as pltpu
from jax.sharding import PartitionSpec as P

LANES = 128
GROUPS = 8
MIB = 1024 * 1024


MESH = pl.DeviceIdType.MESH


def slab_lanes(slab):
    return pl.ds(pl.multiple_of(slab * LANES, LANES), LANES)


def wide(row):
    return jnp.broadcast_to(row, (GROUPS, LANES))


def first_pass(slab, keep, steps, modes, halo, projected, taps, rate, extended, queries, product, starts, ends):
    lanes = slab_lanes(slab)
    bands = starts.shape[0]
    count = steps * GROUPS
    for c in range(3):
        extended[c, pl.ds(6, 2), :] = halo[pl.ds(2 * c, 2), lanes] * keep
        extended[c, pl.ds(8, bands * count), :] = projected[c, :, lanes].astype(jnp.float32)
    speed = [wide(rate[pl.ds(m, 1), lanes]) for m in range(modes)]
    decay = [jnp.exp(-speed[m]) for m in range(modes)]
    tap = [[wide(taps[c, pl.ds(j, 1), lanes]) for j in range(3)] for c in range(3)]
    row = lax.broadcasted_iota(jnp.int32, (GROUPS, LANES), 0)
    last = None
    for band in range(bands):
        first = 8 + band * count
        held = [[extended[c, pl.ds(first - j, GROUPS, stride=steps), :] for j in (2, 1)] for c in range(3)]
        initial = [None if last is None else jnp.where(row == 0, last[m], 0.0) for m in range(modes)]
        state = list(initial)
        for i in range(steps):
            featured = []
            for c in range(3):
                now = extended[c, pl.ds(first + i, GROUPS, stride=steps), :]
                featured.append(tap[c][0] * now + tap[c][1] * held[c][1] + tap[c][2] * held[c][0])
                held[c] = [held[c][1], now]
            x = featured[1] * featured[2]
            queries[band * steps + i, :, lanes] = featured[0]
            product[band * steps + i, :, lanes] = x
            for m in range(modes):
                state[m] = x if state[m] is None else decay[m] * state[m] + x
        last = []
        for m in range(modes):
            here = state[m]
            for distance in (1, 2, 4):
                factor = jnp.where(row >= distance, jnp.exp(speed[m] * (-float(steps * distance))), 0.0)
                here = here + factor * pltpu.roll(here, distance, 0)
            ahead = 0.0 if initial[m] is None else initial[m]
            starts[band, m, :, lanes] = jnp.where(row >= 1, pltpu.roll(here, 1, 0), ahead)
            last.append(wide(here[GROUPS - 1 :, :]))
            if band == bands - 1:
                ends[slab, pl.ds(m, 1), :] = here[GROUPS - 1 :, :]


def second_pass(band, slab, steps, modes, queries, product, starts, before, rate, residue, bias, ordered):
    lanes = slab_lanes(slab)
    row = lax.broadcasted_iota(jnp.int32, (GROUPS, LANES), 0)
    position = ((row + band * GROUPS) * steps).astype(jnp.float32)
    decay, weight, state = [], [], []
    for m in range(modes):
        speed = wide(rate[pl.ds(m, 1), lanes])
        decay.append(jnp.exp(-speed))
        weight.append(wide(residue[pl.ds(m, 1), lanes]))
        carried = jnp.exp(-speed * position) * wide(before[slab, pl.ds(m, 1), :])
        state.append(starts[band, m, :, lanes] + carried)
    skip = wide(bias[pl.ds(0, 1), lanes])
    for i in range(steps):
        x = product[band * steps + i, :, lanes]
        total = skip * x
        for m in range(modes):
            state[m] = decay[m] * state[m] + x
            total = total + weight[m] * state[m]
        ordered[pl.ds(i, GROUPS, stride=steps), :] = queries[band * steps + i, :, lanes] * total
    return ordered[...].astype(jnp.bfloat16)


BANDS = 2
BLOCKS = 4
PARTS = 4
CHUNKS = 8
SHARED = 96
SKEW = 4
SCOPE = 4
WAY = -1
PACE = 1
AHEAD = 5
LAG = 2
ORDER = ((44, 0, 0), (44, 0, 1), (46, 0, 2), (48, 1, 0), (50, 1, 1), (52, 1, 2), (52, 0, 3), (52, 1, 3))


def block_kernel(
    ranks,
    steps,
    modes,
    projected_in,
    taps_in,
    rate_in,
    residue_in,
    bias_in,
    out_weight,
    mixed,
    projected,
    taps,
    rate,
    residue,
    bias,
    last,
    extended,
    ordered,
    queries,
    product,
    starts,
    edge,
    halo,
    ends,
    spread,
    back,
    before,
    weight,
    gathered,
    total,
    leaving,
    returned,
    edge_sem,
    ends_sem,
    back_sem,
    left_sem,
    right_sem,
    swap_sem,
    twin_sem,
    sent_sem,
    rows_sem,
    return_sem,
    mixed_sem,
    input_sem,
    rows_in_sem,
):
    rank = lax.axis_index("seq")
    z = lax.axis_index("grp")
    depth = mixed.shape[0]
    rows = projected.shape[1]
    band_rows = steps * GROUPS
    x, y, core = rank // 8, (rank // 2) % 4, rank % 2
    side = y % 2
    q = (x + 2 * (y // 2)) % BLOCKS

    def at(px, py, pcore):
        return (px % 4) * 8 + (py % 4) * 2 + pcore

    x_up, x_down = at(x + 1, y, core), at(x + 3, y, core)
    y_out = at(x, y + 3 + 2 * side, core)
    y_pair = at(x, y + 1 - 2 * side, core)
    twin = at(x, y, 1 - core)

    def remote(source, target, send_sem, recv_sem, to_rank, to_z):
        return pltpu.make_async_remote_copy(
            src_ref=source,
            dst_ref=target,
            send_sem=send_sem,
            recv_sem=recv_sem,
            device_id=(to_rank, to_z),
            device_id_type=MESH,
        )

    groups = ranks // SCOPE
    wide_lanes = SCOPE * LANES

    last_in = pltpu.make_async_copy(projected_in.at[:, pl.ds(rows - 16, 16)], last, input_sem.at[0])
    last_in.start()
    small = [
        pltpu.make_async_copy(source, target, input_sem.at[1 + i])
        for i, (source, target) in enumerate(
            ((taps_in, taps), (rate_in, rate), (residue_in, residue), (bias_in, bias))
        )
    ]
    for copy in small:
        copy.start()

    def rows_in(n):
        lanes = pl.ds(pl.multiple_of(n * wide_lanes, wide_lanes), wide_lanes)
        return pltpu.make_async_copy(
            projected_in.at[:, :, lanes], projected.at[:, :, lanes], rows_in_sem.at[n]
        )

    @pl.loop(0, groups)
    def _(n):
        rows_in(n).start()

    barrier = pltpu.get_barrier_semaphore()

    @pl.loop(1, ranks)
    def _(i):
        pl.semaphore_signal(barrier, inc=1, device_id=(lax.rem(rank + i, ranks), z), device_id_type=MESH)

    @pl.loop(1, depth)
    def _(i):
        pl.semaphore_signal(barrier, inc=1, device_id=(rank, lax.rem(z + i, depth)), device_id_type=MESH)

    up = (WAY * (z - q) + depth) % BLOCKS
    down = (WAY * (q - z) + depth) % BLOCKS
    from_above = ((z + WAY * down + 2 * depth - q) % depth) // BLOCKS
    from_below = 1 - from_above
    span = weight.shape[1] // CHUNKS
    half = span // 2
    taken = half - SHARED
    count = PARTS * CHUNKS

    def weight_rows(j, offset, size, block=None):
        start = pl.multiple_of((j % CHUNKS) * span + core * half + offset, 16)
        columns = pl.ds(0, 2 * LANES) if block is None else slab_lanes(block)
        return weight.at[j // CHUNKS, pl.ds(start, size), columns]

    def moving(j, block, send_sem, recv_sem, to_z):
        view = weight_rows(j, side * SHARED, taken, block)
        return remote(view, view, send_sem, recv_sem.at[j], rank, to_z % depth)

    def upward(j, block):
        return moving(j, block, sent_sem.at[0], left_sem, z + depth + WAY)

    def downward(j, block):
        return moving(j, block, sent_sem.at[1], right_sem, z + depth - WAY)

    def swap(j, block):
        view = weight_rows(j, side * taken, SHARED, block)
        return remote(view, view, sent_sem.at[2], swap_sem.at[j], y_pair, z)

    def weight_step(n):
        j = n - SKEW * down

        @pl.when((j >= 0) & (j < count))
        def _():
            downward(j, from_above).wait_recv()

            @pl.when(down < BLOCKS - 1)
            def _():
                downward(j, from_above).start()

            @pl.when(up == 0)
            def _():
                upward(j, from_above).start()

            swap(j, from_above).start()

        k = n - SKEW * jnp.where(up == 0, BLOCKS, up)

        @pl.when((k >= 0) & (k < count))
        def _():
            upward(k, from_below).wait_recv()

            @pl.when(up > 0)
            def _():
                upward(k, from_below).start()

            swap(k, from_below).start()

        whole = n - SKEW * (BLOCKS + 1)

        @pl.when((whole >= 0) & (whole < count))
        def _():
            other = weight_rows(whole, (1 - side) * taken, SHARED)
            remote(other, other, sent_sem.at[2], swap_sem.at[whole], y_pair, z).wait_recv()
            view = weight_rows(whole, 0, half)
            remote(view, view, sent_sem.at[3], twin_sem.at[whole // CHUNKS], twin, z).start()

    def weight_steps(first, last):
        @pl.loop(first, last)
        def _(n):
            weight_step(n)

    @pl.when(down == 0)
    def _():
        @pl.loop(0, count)
        def _(j):
            start = pl.multiple_of((j % CHUNKS) * span + core * half + side * SHARED, 16)
            pltpu.make_async_copy(
                out_weight.at[pl.ds(start, taken), slab_lanes(j // CHUNKS)],
                weight_rows(j, side * SHARED, taken, from_above),
                right_sem.at[j],
            ).start()

    last_in.wait()
    for c in range(3):
        edge[pl.ds(2 * c, 2), :] = last[c].astype(jnp.float32)[14:, :]
    pl.semaphore_wait(barrier, ranks + depth - 2)

    edge_copy = remote(edge, halo, edge_sem.at[0], edge_sem.at[1], lax.rem(rank + 1, ranks), z)
    edge_copy.start()
    weight_step(0)
    for copy in small:
        copy.wait()
    edge_copy.wait_recv()
    keep = jnp.where(rank > 0, 1.0, 0.0)

    def all_but_one(ref, send_sem, recv_sem):
        view = ref.at[pl.ds(0, ranks - 1)]
        return remote(view, view, send_sem, recv_sem, lax.rem(rank + 1, ranks), z)

    def first_group(n):
        rows_in(n).wait()

        @pl.loop(0, SCOPE)
        def _(i):
            slab = n * SCOPE + (i + rank) % SCOPE
            first_pass(
                slab, keep, steps, modes, halo, projected, taps, rate, extended, queries, product, starts, ends
            )

            @pl.when(slab == rank)
            def _():
                spread[rank] = ends[rank]

            @pl.when(slab != rank)
            def _():
                remote(ends.at[slab], spread.at[rank], ends_sem.at[0], ends_sem.at[1], slab, z).start()

    def scan():
        all_but_one(spread, ends_sem.at[0], ends_sem.at[1]).wait_recv()
        factor = jnp.exp(rate[:, slab_lanes(rank)] * (-float(rows)))
        carried = jnp.zeros_like(factor)
        for r in range(ranks):
            back[r] = carried
            carried = factor * carried + spread[r]
        arrival = back_sem.at[1 + rank // SCOPE]
        pltpu.make_async_copy(back.at[rank], before.at[rank], arrival).start()

        @pl.loop(1, ranks)
        def _(i):
            other = lax.rem(rank + i, ranks)
            remote(back.at[other], before.at[rank], back_sem.at[0], arrival, other, z).start()

    def rows_copy(band, n, slot, to_rank):
        return remote(
            gathered.at[band, n, 0],
            gathered.at[band, n, slot],
            rows_sem.at[0],
            rows_sem.at[3 * band + slot],
            to_rank,
            z,
        )

    def second_group(band, n):
        if band == 0:
            view = before.at[pl.ds(n * SCOPE, SCOPE)]
            remote(view, view, back_sem.at[0], back_sem.at[1 + n], x_up, z).wait_recv()

        @pl.loop(0, SCOPE)
        def _(i):
            gathered[band, n, 0, :, slab_lanes(i)] = second_pass(
                band, n * SCOPE + i, steps, modes, queries, product, starts, before, rate, residue, bias, ordered
            )

        rows_copy(band, n, 1, x_up).start()
        rows_copy(band, n, 2, x_down).start()
        rows_copy(band, n, 3, y_out).start()

    @pl.loop(0, groups)
    def _(n):
        for i in range(PACE):
            weight_step(n * PACE + 1 + i)
        first_group((n + rank // SCOPE) % groups)

    step = 1 + PACE * groups
    weight_steps(step, step + AHEAD)
    scan()
    weight_steps(step + AHEAD, step + 2 * AHEAD)

    step = step + 2 * AHEAD
    for band in range(BANDS):

        @pl.loop(0, groups)
        def _(n):
            for i in range(PACE):
                weight_step(n * PACE + step + i)
            second_group(band, n)

        step += PACE * groups

    def return_copy(band, p, i, slot, to_rank):
        return remote(
            leaving.at[band, p, i],
            returned.at[band, p, slot],
            return_sem.at[0],
            return_sem.at[slot + 3 * (p + PARTS * band)],
            to_rank,
            z,
        )

    def project(band, p):
        def term(n):
            block = gathered[band, n].reshape(BLOCKS * band_rows, wide_lanes)
            start = pl.multiple_of(n * wide_lanes, wide_lanes)
            return jnp.dot(block, weight[p, pl.ds(start, wide_lanes), :], preferred_element_type=jnp.float32)

        total[...] = term(0)

        @pl.loop(1, groups)
        def _(n):
            total[...] += term(n)

        for i in range(3):
            leaving[band, p, i] = total[pl.ds((i + 1) * band_rows, band_rows), :].astype(jnp.bfloat16)
        returned[band, p, 0] = total[pl.ds(0, band_rows), :].astype(jnp.bfloat16)
        return_copy(band, p, 0, 2, x_down).start()
        return_copy(band, p, 1, 1, x_up).start()
        return_copy(band, p, 2, 3, y_out).start()

    def deliver(band, p):
        return_copy(band, p, 0, 2, x_down).wait_recv()
        return_copy(band, p, 1, 1, x_up).wait_recv()
        return_copy(band, p, 2, 3, y_out).wait_recv()
        for slot, block in ((0, q), (1, q + 3), (2, q + 1), (3, q + 2)):
            for upper in range(2):
                owner = (block % BLOCKS + BLOCKS * upper) % depth
                view = returned.at[band, p, slot, :, pl.ds(upper * LANES, LANES)]
                target = mixed.at[z, pl.ds(band * band_rows, band_rows), pl.ds(p * LANES, LANES)]

                @pl.when(owner == z)
                def _():
                    target[...] = view[...]

                @pl.when(owner != z)
                def _():
                    remote(view, target, mixed_sem.at[0], mixed_sem.at[1], rank, owner).start()

    waiting = []
    bands_here, parts_here = set(), set()
    for until, band, p in ORDER:
        if until > step:
            weight_steps(step, until)
            step = until
        if band not in bands_here:
            bands_here.add(band)
            for slot in (1, 2, 3):
                view = gathered.at[band, :, slot]
                remote(view, view, rows_sem.at[0], rows_sem.at[3 * band + slot], x_up, z).wait_recv()
        if p not in parts_here:
            parts_here.add(p)
            half_part = weight.at[p, pl.ds(0, weight.shape[1] // 2)]
            remote(half_part, half_part, sent_sem.at[3], twin_sem.at[p], twin, z).wait_recv()
        project(band, p)
        waiting.append((band, p))
        if len(waiting) > LAG:
            deliver(*waiting.pop(0))
    for item in waiting:
        deliver(*item)

    edge_copy.wait_send()
    all_but_one(ends, ends_sem.at[0], ends_sem.at[1]).wait_send()
    all_but_one(back, back_sem.at[0], back_sem.at[1]).wait_send()

    def sent(view, sem):
        remote(view, view, sem, left_sem.at[0], x_up, z).wait_send()

    chain = weight.at[0, pl.ds(0, count * taken // 2)]
    sent(chain, sent_sem.at[0])

    @pl.when(down < BLOCKS - 1)
    def _():
        sent(chain, sent_sem.at[1])

    sent(weight.at[0, pl.ds(0, count * SHARED)], sent_sem.at[2])
    sent(weight.at[pl.ds(0, PARTS // 2)], sent_sem.at[3])
    sent(gathered.at[:, :, pl.ds(0, 3)], rows_sem.at[0])
    sent(leaving, return_sem.at[0])
    others = mixed.at[pl.ds(0, depth - 1)]
    remote(others, others, mixed_sem.at[0], mixed_sem.at[1], x_up, z).wait()


def on_device(projected, short_filter, bias, residue, rate, out_weight):
    ranks = lax.axis_size("seq")
    depth = lax.axis_size("grp")
    taken = projected[:, 0]
    rows, width = taken.shape[1:]
    modes = rate.shape[0]
    steps = rows // (GROUPS * BANDS)
    f32, bf16 = jnp.float32, jnp.bfloat16
    vmem = pl.BlockSpec(memory_space=pltpu.VMEM)
    exchanged = pltpu.VMEM((ranks, modes, width // ranks), f32)
    dma = pltpu.SemaphoreType.DMA
    return pl.pallas_call(
        functools.partial(block_kernel, ranks, steps, modes),
        in_specs=[pl.BlockSpec(memory_space=pl.ANY)] * 6,
        out_specs=vmem,
        out_shape=jax.ShapeDtypeStruct((depth, rows, out_weight.shape[1]), bf16),
        scratch_shapes=[
            pltpu.VMEM(taken.shape, bf16),
            pltpu.VMEM(short_filter.shape, f32),
            pltpu.VMEM(rate.shape, f32),
            pltpu.VMEM(residue.shape, f32),
            pltpu.VMEM((1, width), f32),
            pltpu.VMEM((3, 16, width), bf16),
            pltpu.VMEM((3, rows + 8, LANES), f32),
            pltpu.VMEM((steps * GROUPS, LANES), f32),
            pltpu.VMEM((BANDS * steps, GROUPS, width), f32),
            pltpu.VMEM((BANDS * steps, GROUPS, width), f32),
            pltpu.VMEM((BANDS, modes, GROUPS, width), f32),
            pltpu.VMEM((8, width), f32),
            pltpu.VMEM((8, width), f32),
            exchanged,
            exchanged,
            exchanged,
            exchanged,
            pltpu.VMEM((PARTS, width, 2 * LANES), bf16),
            pltpu.VMEM((BANDS, ranks // SCOPE, BLOCKS, rows // BANDS, SCOPE * LANES), bf16),
            pltpu.VMEM((BLOCKS * rows // BANDS, 2 * LANES), f32),
            pltpu.VMEM((BANDS, PARTS, 3, rows // BANDS, 2 * LANES), bf16),
            pltpu.VMEM((BANDS, PARTS, BLOCKS, rows // BANDS, 2 * LANES), bf16),
            dma((2,)),
            dma((2,)),
            dma((1 + ranks // SCOPE,)),
            dma((PARTS * CHUNKS,)),
            dma((PARTS * CHUNKS,)),
            dma((PARTS * CHUNKS,)),
            dma((PARTS,)),
            dma((4,)),
            dma((1 + 3 * BANDS,)),
            dma((1 + 3 * BANDS * PARTS,)),
            dma((2,)),
            dma((5,)),
            dma((ranks // SCOPE,)),
        ],
        compiler_params=pltpu.CompilerParams(
            collective_id=0, has_side_effects=True, vmem_limit_bytes=48 * MIB
        ),
    )(taken, short_filter, rate, residue, bias[None], out_weight)


def solution(mesh):
    placed = (P(None, "grp", "seq", None), P(), P(), P(), P(), P(None, "grp"))
    return jax.shard_map(
        on_device, mesh=mesh, in_specs=placed, out_specs=P(None, "seq", "grp"), check_vma=False
    )
```

```python
import functools

import jax
import jax.numpy as jnp
from jax import lax
from jax.experimental import pallas as pl
from jax.experimental.pallas import tpu as pltpu
from jax.sharding import PartitionSpec as P

LANES = 128
GROUPS = 8
MIB = 1024 * 1024


MESH = pl.DeviceIdType.MESH


def slab_lanes(slab):
    return pl.ds(pl.multiple_of(slab * LANES, LANES), LANES)


def wide(row):
    return jnp.broadcast_to(row, (GROUPS, LANES))


def first_pass(slab, keep, steps, modes, halo, projected, taps, rate, extended, queries, product, starts, ends):
    lanes = slab_lanes(slab)
    bands = starts.shape[0]
    count = steps * GROUPS
    for c in range(3):
        extended[c, pl.ds(6, 2), :] = halo[pl.ds(2 * c, 2), lanes] * keep
        extended[c, pl.ds(8, bands * count), :] = projected[c, :, lanes].astype(jnp.float32)
    speed = [wide(rate[pl.ds(m, 1), lanes]) for m in range(modes)]
    decay = [jnp.exp(-speed[m]) for m in range(modes)]
    tap = [[wide(taps[c, pl.ds(j, 1), lanes]) for j in range(3)] for c in range(3)]
    row = lax.broadcasted_iota(jnp.int32, (GROUPS, LANES), 0)
    last = None
    for band in range(bands):
        first = 8 + band * count
        held = [[extended[c, pl.ds(first - j, GROUPS, stride=steps), :] for j in (2, 1)] for c in range(3)]
        initial = [None if last is None else jnp.where(row == 0, last[m], 0.0) for m in range(modes)]
        state = list(initial)
        for i in range(steps):
            featured = []
            for c in range(3):
                now = extended[c, pl.ds(first + i, GROUPS, stride=steps), :]
                featured.append(tap[c][0] * now + tap[c][1] * held[c][1] + tap[c][2] * held[c][0])
                held[c] = [held[c][1], now]
            x = featured[1] * featured[2]
            queries[band * steps + i, :, lanes] = featured[0]
            product[band * steps + i, :, lanes] = x
            for m in range(modes):
                state[m] = x if state[m] is None else decay[m] * state[m] + x
        last = []
        for m in range(modes):
            here = state[m]
            for distance in (1, 2, 4):
                factor = jnp.where(row >= distance, jnp.exp(speed[m] * (-float(steps * distance))), 0.0)
                here = here + factor * pltpu.roll(here, distance, 0)
            ahead = 0.0 if initial[m] is None else initial[m]
            starts[band, m, :, lanes] = jnp.where(row >= 1, pltpu.roll(here, 1, 0), ahead)
            last.append(wide(here[GROUPS - 1 :, :]))
            if band == bands - 1:
                ends[slab, pl.ds(m, 1), :] = here[GROUPS - 1 :, :]


def second_pass(band, slab, steps, modes, queries, product, starts, before, rate, residue, bias, ordered):
    lanes = slab_lanes(slab)
    row = lax.broadcasted_iota(jnp.int32, (GROUPS, LANES), 0)
    position = ((row + band * GROUPS) * steps).astype(jnp.float32)
    decay, weight, state = [], [], []
    for m in range(modes):
        speed = wide(rate[pl.ds(m, 1), lanes])
        decay.append(jnp.exp(-speed))
        weight.append(wide(residue[pl.ds(m, 1), lanes]))
        carried = jnp.exp(-speed * position) * wide(before[slab, pl.ds(m, 1), :])
        state.append(starts[band, m, :, lanes] + carried)
    skip = wide(bias[pl.ds(0, 1), lanes])
    for i in range(steps):
        x = product[band * steps + i, :, lanes]
        total = skip * x
        for m in range(modes):
            state[m] = decay[m] * state[m] + x
            total = total + weight[m] * state[m]
        ordered[pl.ds(i, GROUPS, stride=steps), :] = queries[band * steps + i, :, lanes] * total
    return ordered[...].astype(jnp.bfloat16)


BANDS = 2
BLOCKS = 4
PARTS = 4
CHUNKS = 8
SHARED = 96
SKEW = 4
SCOPE = 4
WAY = -1
PACE = 1
AHEAD = 5
LAG = 2
ORDER = ((40, 0, 0), (42, 0, 1), (44, 0, 2), (48, 1, 0), (50, 1, 1), (52, 1, 2), (52, 0, 3), (52, 1, 3))


def block_kernel(
    ranks,
    steps,
    modes,
    projected_in,
    taps_in,
    rate_in,
    residue_in,
    bias_in,
    out_weight,
    mixed,
    projected,
    taps,
    rate,
    residue,
    bias,
    last,
    extended,
    ordered,
    queries,
    product,
    starts,
    edge,
    halo,
    ends,
    spread,
    back,
    before,
    weight,
    gathered,
    total,
    leaving,
    returned,
    edge_sem,
    ends_sem,
    back_sem,
    left_sem,
    right_sem,
    swap_sem,
    twin_sem,
    sent_sem,
    rows_sem,
    return_sem,
    mixed_sem,
    input_sem,
    rows_in_sem,
):
    rank = lax.axis_index("seq")
    z = lax.axis_index("grp")
    depth = mixed.shape[0]
    rows = projected.shape[1]
    band_rows = steps * GROUPS
    x, y, core = rank // 8, (rank // 2) % 4, rank % 2
    side = y % 2
    q = (x + 2 * (y // 2)) % BLOCKS

    def at(px, py, pcore):
        return (px % 4) * 8 + (py % 4) * 2 + pcore

    x_up, x_down = at(x + 1, y, core), at(x + 3, y, core)
    y_out = at(x, y + 3 + 2 * side, core)
    y_pair = at(x, y + 1 - 2 * side, core)
    twin = at(x, y, 1 - core)

    def remote(source, target, send_sem, recv_sem, to_rank, to_z):
        return pltpu.make_async_remote_copy(
            src_ref=source,
            dst_ref=target,
            send_sem=send_sem,
            recv_sem=recv_sem,
            device_id=(to_rank, to_z),
            device_id_type=MESH,
        )

    groups = ranks // SCOPE
    wide_lanes = SCOPE * LANES

    last_in = pltpu.make_async_copy(projected_in.at[:, pl.ds(rows - 16, 16)], last, input_sem.at[0])
    last_in.start()
    small = [
        pltpu.make_async_copy(source, target, input_sem.at[1 + i])
        for i, (source, target) in enumerate(
            ((taps_in, taps), (rate_in, rate), (residue_in, residue), (bias_in, bias))
        )
    ]
    for copy in small:
        copy.start()

    def rows_in(n):
        lanes = pl.ds(pl.multiple_of(n * wide_lanes, wide_lanes), wide_lanes)
        return pltpu.make_async_copy(
            projected_in.at[:, :, lanes], projected.at[:, :, lanes], rows_in_sem.at[n]
        )

    @pl.loop(0, groups)
    def _(n):
        rows_in(n).start()

    barrier = pltpu.get_barrier_semaphore()

    @pl.loop(1, ranks)
    def _(i):
        pl.semaphore_signal(barrier, inc=1, device_id=(lax.rem(rank + i, ranks), z), device_id_type=MESH)

    @pl.loop(1, depth)
    def _(i):
        pl.semaphore_signal(barrier, inc=1, device_id=(rank, lax.rem(z + i, depth)), device_id_type=MESH)

    up = (WAY * (z - q) + depth) % BLOCKS
    down = (WAY * (q - z) + depth) % BLOCKS
    from_above = ((z + WAY * down + 2 * depth - q) % depth) // BLOCKS
    from_below = 1 - from_above
    span = weight.shape[1] // CHUNKS
    half = span // 2
    taken = half - SHARED
    count = PARTS * CHUNKS

    def weight_rows(j, offset, size, block=None):
        start = pl.multiple_of((j % CHUNKS) * span + core * half + offset, 16)
        columns = pl.ds(0, 2 * LANES) if block is None else slab_lanes(block)
        return weight.at[j // CHUNKS, pl.ds(start, size), columns]

    def moving(j, block, send_sem, recv_sem, to_z):
        view = weight_rows(j, side * SHARED, taken, block)
        return remote(view, view, send_sem, recv_sem.at[j], rank, to_z % depth)

    def upward(j, block):
        return moving(j, block, sent_sem.at[0], left_sem, z + depth + WAY)

    def downward(j, block):
        return moving(j, block, sent_sem.at[1], right_sem, z + depth - WAY)

    def swap(j, block):
        view = weight_rows(j, side * taken, SHARED, block)
        return remote(view, view, sent_sem.at[2], swap_sem.at[j], y_pair, z)

    def weight_step(n):
        j = n - SKEW * down

        @pl.when((j >= 0) & (j < count))
        def _():
            downward(j, from_above).wait_recv()

            @pl.when(down < BLOCKS - 1)
            def _():
                downward(j, from_above).start()

            @pl.when(up == 0)
            def _():
                upward(j, from_above).start()

            swap(j, from_above).start()

        k = n - SKEW * jnp.where(up == 0, BLOCKS, up)

        @pl.when((k >= 0) & (k < count))
        def _():
            upward(k, from_below).wait_recv()

            @pl.when(up > 0)
            def _():
                upward(k, from_below).start()

            swap(k, from_below).start()

        whole = n - SKEW * (BLOCKS + 1)

        @pl.when((whole >= 0) & (whole < count))
        def _():
            other = weight_rows(whole, (1 - side) * taken, SHARED)
            remote(other, other, sent_sem.at[2], swap_sem.at[whole], y_pair, z).wait_recv()
            view = weight_rows(whole, 0, half)
            remote(view, view, sent_sem.at[3], twin_sem.at[whole // CHUNKS], twin, z).start()

    def weight_steps(first, last):
        @pl.loop(first, last)
        def _(n):
            weight_step(n)

    @pl.when(down == 0)
    def _():
        @pl.loop(0, count)
        def _(j):
            start = pl.multiple_of((j % CHUNKS) * span + core * half + side * SHARED, 16)
            pltpu.make_async_copy(
                out_weight.at[pl.ds(start, taken), slab_lanes(j // CHUNKS)],
                weight_rows(j, side * SHARED, taken, from_above),
                right_sem.at[j],
            ).start()

    last_in.wait()
    for c in range(3):
        edge[pl.ds(2 * c, 2), :] = last[c].astype(jnp.float32)[14:, :]
    pl.semaphore_wait(barrier, ranks + depth - 2)

    edge_copy = remote(edge, halo, edge_sem.at[0], edge_sem.at[1], lax.rem(rank + 1, ranks), z)
    edge_copy.start()
    weight_step(0)
    for copy in small:
        copy.wait()
    edge_copy.wait_recv()
    keep = jnp.where(rank > 0, 1.0, 0.0)

    def all_but_one(ref, send_sem, recv_sem):
        view = ref.at[pl.ds(0, ranks - 1)]
        return remote(view, view, send_sem, recv_sem, lax.rem(rank + 1, ranks), z)

    def first_group(n):
        rows_in(n).wait()

        @pl.loop(0, SCOPE)
        def _(i):
            slab = n * SCOPE + (i + rank) % SCOPE
            first_pass(
                slab, keep, steps, modes, halo, projected, taps, rate, extended, queries, product, starts, ends
            )

            @pl.when(slab == rank)
            def _():
                spread[rank] = ends[rank]

            @pl.when(slab != rank)
            def _():
                remote(ends.at[slab], spread.at[rank], ends_sem.at[0], ends_sem.at[1], slab, z).start()

    def scan():
        all_but_one(spread, ends_sem.at[0], ends_sem.at[1]).wait_recv()
        factor = jnp.exp(rate[:, slab_lanes(rank)] * (-float(rows)))
        carried = jnp.zeros_like(factor)
        for r in range(ranks):
            back[r] = carried
            carried = factor * carried + spread[r]
        arrival = back_sem.at[1 + rank // SCOPE]
        pltpu.make_async_copy(back.at[rank], before.at[rank], arrival).start()

        @pl.loop(1, ranks)
        def _(i):
            other = lax.rem(rank + i, ranks)
            remote(back.at[other], before.at[rank], back_sem.at[0], arrival, other, z).start()

    def rows_copy(band, n, slot, to_rank):
        return remote(
            gathered.at[band, n, 0],
            gathered.at[band, n, slot],
            rows_sem.at[0],
            rows_sem.at[3 * band + slot],
            to_rank,
            z,
        )

    def second_group(band, n):
        if band == 0:
            view = before.at[pl.ds(n * SCOPE, SCOPE)]
            remote(view, view, back_sem.at[0], back_sem.at[1 + n], x_up, z).wait_recv()

        @pl.loop(0, SCOPE)
        def _(i):
            gathered[band, n, 0, :, slab_lanes(i)] = second_pass(
                band, n * SCOPE + i, steps, modes, queries, product, starts, before, rate, residue, bias, ordered
            )

        rows_copy(band, n, 1, x_up).start()
        rows_copy(band, n, 2, x_down).start()
        rows_copy(band, n, 3, y_out).start()

    @pl.loop(0, groups)
    def _(n):
        for i in range(PACE):
            weight_step(n * PACE + 1 + i)
        first_group((n + rank // SCOPE) % groups)

    step = 1 + PACE * groups
    weight_steps(step, step + AHEAD)
    scan()
    weight_steps(step + AHEAD, step + 2 * AHEAD)

    step = step + 2 * AHEAD
    for band in range(BANDS):

        @pl.loop(0, groups)
        def _(n):
            for i in range(PACE):
                weight_step(n * PACE + step + i)
            second_group(band, n)

        step += PACE * groups

    def return_copy(band, p, i, slot, to_rank):
        return remote(
            leaving.at[band, p, i],
            returned.at[band, p, slot],
            return_sem.at[0],
            return_sem.at[slot + 3 * (p + PARTS * band)],
            to_rank,
            z,
        )

    def project(band, p):
        def term(n):
            block = gathered[band, n].reshape(BLOCKS * band_rows, wide_lanes)
            start = pl.multiple_of(n * wide_lanes, wide_lanes)
            return jnp.dot(block, weight[p, pl.ds(start, wide_lanes), :], preferred_element_type=jnp.float32)

        total[...] = term(0)

        @pl.loop(1, groups)
        def _(n):
            total[...] += term(n)

        for i in range(3):
            leaving[band, p, i] = total[pl.ds((i + 1) * band_rows, band_rows), :].astype(jnp.bfloat16)
        returned[band, p, 0] = total[pl.ds(0, band_rows), :].astype(jnp.bfloat16)
        return_copy(band, p, 0, 2, x_down).start()
        return_copy(band, p, 1, 1, x_up).start()
        return_copy(band, p, 2, 3, y_out).start()

    def deliver(band, p):
        return_copy(band, p, 0, 2, x_down).wait_recv()
        return_copy(band, p, 1, 1, x_up).wait_recv()
        return_copy(band, p, 2, 3, y_out).wait_recv()
        for slot, block in ((0, q), (1, q + 3), (2, q + 1), (3, q + 2)):
            for upper in range(2):
                owner = (block % BLOCKS + BLOCKS * upper) % depth
                view = returned.at[band, p, slot, :, pl.ds(upper * LANES, LANES)]
                target = mixed.at[z, pl.ds(band * band_rows, band_rows), pl.ds(p * LANES, LANES)]

                @pl.when(owner == z)
                def _():
                    target[...] = view[...]

                @pl.when(owner != z)
                def _():
                    remote(view, target, mixed_sem.at[0], mixed_sem.at[1], rank, owner).start()

    waiting = []
    bands_here, parts_here = set(), set()
    for until, band, p in ORDER:
        if until > step:
            weight_steps(step, until)
            step = until
        if band not in bands_here:
            bands_here.add(band)
            for slot in (1, 2, 3):
                view = gathered.at[band, :, slot]
                remote(view, view, rows_sem.at[0], rows_sem.at[3 * band + slot], x_up, z).wait_recv()
        if p not in parts_here:
            parts_here.add(p)
            half_part = weight.at[p, pl.ds(0, weight.shape[1] // 2)]
            remote(half_part, half_part, sent_sem.at[3], twin_sem.at[p], twin, z).wait_recv()
        project(band, p)
        waiting.append((band, p))
        if len(waiting) > LAG:
            deliver(*waiting.pop(0))
    for item in waiting:
        deliver(*item)

    edge_copy.wait_send()
    all_but_one(ends, ends_sem.at[0], ends_sem.at[1]).wait_send()
    all_but_one(back, back_sem.at[0], back_sem.at[1]).wait_send()

    def sent(view, sem):
        remote(view, view, sem, left_sem.at[0], x_up, z).wait_send()

    chain = weight.at[0, pl.ds(0, count * taken // 2)]
    sent(chain, sent_sem.at[0])

    @pl.when(down < BLOCKS - 1)
    def _():
        sent(chain, sent_sem.at[1])

    sent(weight.at[0, pl.ds(0, count * SHARED)], sent_sem.at[2])
    sent(weight.at[pl.ds(0, PARTS // 2)], sent_sem.at[3])
    sent(gathered.at[:, :, pl.ds(0, 3)], rows_sem.at[0])
    sent(leaving, return_sem.at[0])
    others = mixed.at[pl.ds(0, depth - 1)]
    remote(others, others, mixed_sem.at[0], mixed_sem.at[1], x_up, z).wait()


def on_device(projected, short_filter, bias, residue, rate, out_weight):
    ranks = lax.axis_size("seq")
    depth = lax.axis_size("grp")
    taken = projected[:, 0]
    rows, width = taken.shape[1:]
    modes = rate.shape[0]
    steps = rows // (GROUPS * BANDS)
    f32, bf16 = jnp.float32, jnp.bfloat16
    vmem = pl.BlockSpec(memory_space=pltpu.VMEM)
    exchanged = pltpu.VMEM((ranks, modes, width // ranks), f32)
    dma = pltpu.SemaphoreType.DMA
    return pl.pallas_call(
        functools.partial(block_kernel, ranks, steps, modes),
        in_specs=[pl.BlockSpec(memory_space=pl.ANY)] * 6,
        out_specs=vmem,
        out_shape=jax.ShapeDtypeStruct((depth, rows, out_weight.shape[1]), bf16),
        scratch_shapes=[
            pltpu.VMEM(taken.shape, bf16),
            pltpu.VMEM(short_filter.shape, f32),
            pltpu.VMEM(rate.shape, f32),
            pltpu.VMEM(residue.shape, f32),
            pltpu.VMEM((1, width), f32),
            pltpu.VMEM((3, 16, width), bf16),
            pltpu.VMEM((3, rows + 8, LANES), f32),
            pltpu.VMEM((steps * GROUPS, LANES), f32),
            pltpu.VMEM((BANDS * steps, GROUPS, width), f32),
            pltpu.VMEM((BANDS * steps, GROUPS, width), f32),
            pltpu.VMEM((BANDS, modes, GROUPS, width), f32),
            pltpu.VMEM((8, width), f32),
            pltpu.VMEM((8, width), f32),
            exchanged,
            exchanged,
            exchanged,
            exchanged,
            pltpu.VMEM((PARTS, width, 2 * LANES), bf16),
            pltpu.VMEM((BANDS, ranks // SCOPE, BLOCKS, rows // BANDS, SCOPE * LANES), bf16),
            pltpu.VMEM((BLOCKS * rows // BANDS, 2 * LANES), f32),
            pltpu.VMEM((BANDS, PARTS, 3, rows // BANDS, 2 * LANES), bf16),
            pltpu.VMEM((BANDS, PARTS, BLOCKS, rows // BANDS, 2 * LANES), bf16),
            dma((2,)),
            dma((2,)),
            dma((1 + ranks // SCOPE,)),
            dma((PARTS * CHUNKS,)),
            dma((PARTS * CHUNKS,)),
            dma((PARTS * CHUNKS,)),
            dma((PARTS,)),
            dma((4,)),
            dma((1 + 3 * BANDS,)),
            dma((1 + 3 * BANDS * PARTS,)),
            dma((2,)),
            dma((5,)),
            dma((ranks // SCOPE,)),
        ],
        compiler_params=pltpu.CompilerParams(
            collective_id=0, has_side_effects=True, vmem_limit_bytes=62 * MIB
        ),
    )(taken, short_filter, rate, residue, bias[None], out_weight)


def solution(mesh):
    placed = (P(None, "grp", "seq", None), P(), P(), P(), P(), P(None, "grp"))
    return jax.shard_map(
        on_device, mesh=mesh, in_specs=placed, out_specs=P(None, "seq", "grp"), check_vma=False
    )
```

```python
import functools

import jax
import jax.numpy as jnp
from jax import lax
from jax.experimental import pallas as pl
from jax.experimental.pallas import tpu as pltpu
from jax.sharding import PartitionSpec as P

LANES = 128
GROUPS = 8
MIB = 1024 * 1024


MESH = pl.DeviceIdType.MESH


def slab_lanes(slab):
    return pl.ds(pl.multiple_of(slab * LANES, LANES), LANES)


def wide(row):
    return jnp.broadcast_to(row, (GROUPS, LANES))


def first_pass(band, slab, keep, steps, modes, halo, projected, taps, rate, extended, queries, product, starts, middle, ends):
    lanes = slab_lanes(slab)
    count = steps * GROUPS
    first = 8 + band * count
    ahead = 16 * band
    for c in range(3):
        if band == 0:
            extended[c, pl.ds(6, 2), :] = halo[pl.ds(2 * c, 2), lanes] * keep
        extended[c, pl.ds(first - ahead, count + ahead), :] = projected[
            c, pl.ds(band * count - ahead, count + ahead), lanes
        ].astype(jnp.float32)
    speed = [wide(rate[pl.ds(m, 1), lanes]) for m in range(modes)]
    decay = [jnp.exp(-speed[m]) for m in range(modes)]
    tap = [[wide(taps[c, pl.ds(j, 1), lanes]) for j in range(3)] for c in range(3)]
    row = lax.broadcasted_iota(jnp.int32, (GROUPS, LANES), 0)
    held = [[extended[c, pl.ds(first - j, GROUPS, stride=steps), :] for j in (2, 1)] for c in range(3)]
    state = [None] * modes
    for i in range(steps):
        featured = []
        for c in range(3):
            now = extended[c, pl.ds(first + i, GROUPS, stride=steps), :]
            featured.append(tap[c][0] * now + tap[c][1] * held[c][1] + tap[c][2] * held[c][0])
            held[c] = [held[c][1], now]
        x = featured[1] * featured[2]
        queries[band * steps + i, :, lanes] = featured[0]
        product[band * steps + i, :, lanes] = x
        for m in range(modes):
            state[m] = x if i == 0 else decay[m] * state[m] + x
    for m in range(modes):
        here = state[m]
        for distance in (1, 2, 4):
            factor = jnp.where(row >= distance, jnp.exp(speed[m] * (-float(steps * distance))), 0.0)
            here = here + factor * pltpu.roll(here, distance, 0)
        starts[band, m, :, lanes] = jnp.where(row >= 1, pltpu.roll(here, 1, 0), 0.0)
        last = here[GROUPS - 1 :, :]
        if band:
            ends[slab, pl.ds(m, 1), :] = last
        else:
            middle[slab, pl.ds(m, 1), :] = last
            across = jnp.exp(rate[pl.ds(m, 1), lanes] * (-float(count)))
            ends[slab, pl.ds(m, 1), :] = ends[slab, pl.ds(m, 1), :] + across * last


def second_pass(band, slab, steps, modes, queries, product, starts, middle, before, rate, residue, bias, ordered):
    lanes = slab_lanes(slab)
    row = lax.broadcasted_iota(jnp.int32, (GROUPS, LANES), 0)
    position = (row * steps).astype(jnp.float32)
    decay, weight, state = [], [], []
    for m in range(modes):
        speed = wide(rate[pl.ds(m, 1), lanes])
        decay.append(jnp.exp(-speed))
        weight.append(wide(residue[pl.ds(m, 1), lanes]))
        entering = before[slab, pl.ds(m, 1), :]
        if band:
            across = jnp.exp(rate[pl.ds(m, 1), lanes] * (-float(steps * GROUPS)))
            entering = across * entering + middle[slab, pl.ds(m, 1), :]
        carried = jnp.exp(-speed * position) * wide(entering)
        state.append(starts[band, m, :, lanes] + carried)
    skip = wide(bias[pl.ds(0, 1), lanes])
    for i in range(steps):
        x = product[band * steps + i, :, lanes]
        total = skip * x
        for m in range(modes):
            state[m] = decay[m] * state[m] + x
            total = total + weight[m] * state[m]
        ordered[pl.ds(i, GROUPS, stride=steps), :] = queries[band * steps + i, :, lanes] * total
    return ordered[...].astype(jnp.bfloat16)


BANDS = 2
BLOCKS = 4
PARTS = 4
CHUNKS = 8
SHARED = 96
SKEW = 4
SCOPE = 4
WAY = -1
PACE = 1
AHEAD = 5
LAG = 2
ORDER = ((40, 0, 0), (42, 0, 1), (44, 0, 2), (48, 1, 0), (50, 1, 1), (52, 1, 2), (52, 0, 3), (52, 1, 3))


def block_kernel(
    ranks,
    steps,
    modes,
    projected_in,
    taps_in,
    rate_in,
    residue_in,
    bias_in,
    out_weight,
    mixed,
    projected,
    taps,
    rate,
    residue,
    bias,
    last,
    extended,
    ordered,
    queries,
    product,
    starts,
    middle,
    edge,
    halo,
    ends,
    spread,
    back,
    before,
    weight,
    gathered,
    total,
    leaving,
    returned,
    edge_sem,
    ends_sem,
    back_sem,
    left_sem,
    right_sem,
    swap_sem,
    twin_sem,
    sent_sem,
    rows_sem,
    return_sem,
    mixed_sem,
    input_sem,
    rows_in_sem,
):
    rank = lax.axis_index("seq")
    z = lax.axis_index("grp")
    depth = mixed.shape[0]
    rows = projected.shape[1]
    band_rows = steps * GROUPS
    x, y, core = rank // 8, (rank // 2) % 4, rank % 2
    side = y % 2
    q = (x + 2 * (y // 2)) % BLOCKS

    def at(px, py, pcore):
        return (px % 4) * 8 + (py % 4) * 2 + pcore

    x_up, x_down = at(x + 1, y, core), at(x + 3, y, core)
    y_out = at(x, y + 3 + 2 * side, core)
    y_pair = at(x, y + 1 - 2 * side, core)
    twin = at(x, y, 1 - core)

    def remote(source, target, send_sem, recv_sem, to_rank, to_z):
        return pltpu.make_async_remote_copy(
            src_ref=source,
            dst_ref=target,
            send_sem=send_sem,
            recv_sem=recv_sem,
            device_id=(to_rank, to_z),
            device_id_type=MESH,
        )

    groups = ranks // SCOPE
    wide_lanes = SCOPE * LANES

    last_in = pltpu.make_async_copy(projected_in.at[:, pl.ds(rows - 16, 16)], last, input_sem.at[0])
    last_in.start()
    small = [
        pltpu.make_async_copy(source, target, input_sem.at[1 + i])
        for i, (source, target) in enumerate(
            ((taps_in, taps), (rate_in, rate), (residue_in, residue), (bias_in, bias))
        )
    ]
    for copy in small:
        copy.start()

    def rows_in(n):
        lanes = pl.ds(pl.multiple_of(n * wide_lanes, wide_lanes), wide_lanes)
        return pltpu.make_async_copy(
            projected_in.at[:, :, lanes], projected.at[:, :, lanes], rows_in_sem.at[n]
        )

    @pl.loop(0, groups)
    def _(n):
        rows_in(n).start()

    barrier = pltpu.get_barrier_semaphore()

    @pl.loop(1, ranks)
    def _(i):
        pl.semaphore_signal(barrier, inc=1, device_id=(lax.rem(rank + i, ranks), z), device_id_type=MESH)

    @pl.loop(1, depth)
    def _(i):
        pl.semaphore_signal(barrier, inc=1, device_id=(rank, lax.rem(z + i, depth)), device_id_type=MESH)

    up = (WAY * (z - q) + depth) % BLOCKS
    down = (WAY * (q - z) + depth) % BLOCKS
    from_above = ((z + WAY * down + 2 * depth - q) % depth) // BLOCKS
    from_below = 1 - from_above
    span = weight.shape[1] // CHUNKS
    half = span // 2
    taken = half - SHARED
    count = PARTS * CHUNKS

    def weight_rows(j, offset, size, block=None):
        start = pl.multiple_of((j % CHUNKS) * span + core * half + offset, 16)
        columns = pl.ds(0, 2 * LANES) if block is None else slab_lanes(block)
        return weight.at[j // CHUNKS, pl.ds(start, size), columns]

    def moving(j, block, send_sem, recv_sem, to_z):
        view = weight_rows(j, side * SHARED, taken, block)
        return remote(view, view, send_sem, recv_sem.at[j], rank, to_z % depth)

    def upward(j, block):
        return moving(j, block, sent_sem.at[0], left_sem, z + depth + WAY)

    def downward(j, block):
        return moving(j, block, sent_sem.at[1], right_sem, z + depth - WAY)

    def swap(j, block):
        view = weight_rows(j, side * taken, SHARED, block)
        return remote(view, view, sent_sem.at[2], swap_sem.at[j], y_pair, z)

    def weight_step(n):
        j = n - SKEW * down

        @pl.when((j >= 0) & (j < count))
        def _():
            downward(j, from_above).wait_recv()

            @pl.when(down < BLOCKS - 1)
            def _():
                downward(j, from_above).start()

            @pl.when(up == 0)
            def _():
                upward(j, from_above).start()

            swap(j, from_above).start()

        k = n - SKEW * jnp.where(up == 0, BLOCKS, up)

        @pl.when((k >= 0) & (k < count))
        def _():
            upward(k, from_below).wait_recv()

            @pl.when(up > 0)
            def _():
                upward(k, from_below).start()

            swap(k, from_below).start()

        whole = n - SKEW * (BLOCKS + 1)

        @pl.when((whole >= 0) & (whole < count))
        def _():
            other = weight_rows(whole, (1 - side) * taken, SHARED)
            remote(other, other, sent_sem.at[2], swap_sem.at[whole], y_pair, z).wait_recv()
            view = weight_rows(whole, 0, half)
            remote(view, view, sent_sem.at[3], twin_sem.at[whole // CHUNKS], twin, z).start()

    def weight_steps(first, last):
        @pl.loop(first, last)
        def _(n):
            weight_step(n)

    @pl.when(down == 0)
    def _():
        @pl.loop(0, count)
        def _(j):
            start = pl.multiple_of((j % CHUNKS) * span + core * half + side * SHARED, 16)
            pltpu.make_async_copy(
                out_weight.at[pl.ds(start, taken), slab_lanes(j // CHUNKS)],
                weight_rows(j, side * SHARED, taken, from_above),
                right_sem.at[j],
            ).start()

    last_in.wait()
    for c in range(3):
        edge[pl.ds(2 * c, 2), :] = last[c].astype(jnp.float32)[14:, :]
    pl.semaphore_wait(barrier, ranks + depth - 2)

    edge_copy = remote(edge, halo, edge_sem.at[0], edge_sem.at[1], lax.rem(rank + 1, ranks), z)
    edge_copy.start()
    weight_step(0)
    for copy in small:
        copy.wait()
    keep = jnp.where(rank > 0, 1.0, 0.0)

    def passed(band, slab):
        first_pass(
            band,
            slab,
            keep,
            steps,
            modes,
            halo,
            projected,
            taps,
            rate,
            extended,
            queries,
            product,
            starts,
            middle,
            ends,
        )

    @pl.loop(0, groups)
    def _(n):
        rows_in(n).wait()

        @pl.when(n % 2 == 0)
        def _():
            weight_step(1 + n // 2)

        @pl.loop(0, SCOPE)
        def _(i):
            passed(1, n * SCOPE + i)

    edge_copy.wait_recv()

    def all_but_one(ref, send_sem, recv_sem):
        view = ref.at[pl.ds(0, ranks - 1)]
        return remote(view, view, send_sem, recv_sem, lax.rem(rank + 1, ranks), z)

    def first_group(n):
        @pl.loop(0, SCOPE)
        def _(i):
            slab = n * SCOPE + (i + rank) % SCOPE
            passed(0, slab)

            @pl.when(slab == rank)
            def _():
                spread[rank] = ends[rank]

            @pl.when(slab != rank)
            def _():
                remote(ends.at[slab], spread.at[rank], ends_sem.at[0], ends_sem.at[1], slab, z).start()

    def scan():
        all_but_one(spread, ends_sem.at[0], ends_sem.at[1]).wait_recv()
        factor = jnp.exp(rate[:, slab_lanes(rank)] * (-float(rows)))
        carried = jnp.zeros_like(factor)
        for r in range(ranks):
            back[r] = carried
            carried = factor * carried + spread[r]
        arrival = back_sem.at[1 + rank // SCOPE]
        pltpu.make_async_copy(back.at[rank], before.at[rank], arrival).start()

        @pl.loop(1, ranks)
        def _(i):
            other = lax.rem(rank + i, ranks)
            remote(back.at[other], before.at[rank], back_sem.at[0], arrival, other, z).start()

    def rows_copy(band, n, slot, to_rank):
        return remote(
            gathered.at[band, n, 0],
            gathered.at[band, n, slot],
            rows_sem.at[0],
            rows_sem.at[3 * band + slot],
            to_rank,
            z,
        )

    def second_group(band, n):
        if band == 0:
            view = before.at[pl.ds(n * SCOPE, SCOPE)]
            remote(view, view, back_sem.at[0], back_sem.at[1 + n], x_up, z).wait_recv()

        @pl.loop(0, SCOPE)
        def _(i):
            gathered[band, n, 0, :, slab_lanes(i)] = second_pass(
                band, n * SCOPE + i, steps, modes, queries, product, starts, middle, before, rate, residue, bias, ordered
            )

        rows_copy(band, n, 1, x_up).start()
        rows_copy(band, n, 2, x_down).start()
        rows_copy(band, n, 3, y_out).start()

    @pl.loop(0, groups)
    def _(n):
        @pl.when(n % 2 == 0)
        def _():
            weight_step(1 + groups // 2 + n // 2)

        first_group((n + rank // SCOPE) % groups)

    step = 1 + groups
    weight_steps(step, step + AHEAD)
    scan()
    weight_steps(step + AHEAD, step + 2 * AHEAD)

    step = step + 2 * AHEAD
    for band in range(BANDS):

        @pl.loop(0, groups)
        def _(n):
            for i in range(PACE):
                weight_step(n * PACE + step + i)
            second_group(band, n)

        step += PACE * groups

    def return_copy(band, p, i, slot, to_rank):
        return remote(
            leaving.at[band, p, i],
            returned.at[band, p, slot],
            return_sem.at[0],
            return_sem.at[slot + 3 * (p + PARTS * band)],
            to_rank,
            z,
        )

    def project(band, p):
        def term(n):
            block = gathered[band, n].reshape(BLOCKS * band_rows, wide_lanes)
            start = pl.multiple_of(n * wide_lanes, wide_lanes)
            return jnp.dot(block, weight[p, pl.ds(start, wide_lanes), :], preferred_element_type=jnp.float32)

        total[...] = term(0)

        @pl.loop(1, groups)
        def _(n):
            total[...] += term(n)

        for i in range(3):
            leaving[band, p, i] = total[pl.ds((i + 1) * band_rows, band_rows), :].astype(jnp.bfloat16)
        returned[band, p, 0] = total[pl.ds(0, band_rows), :].astype(jnp.bfloat16)
        return_copy(band, p, 0, 2, x_down).start()
        return_copy(band, p, 1, 1, x_up).start()
        return_copy(band, p, 2, 3, y_out).start()

    def deliver(band, p):
        return_copy(band, p, 0, 2, x_down).wait_recv()
        return_copy(band, p, 1, 1, x_up).wait_recv()
        return_copy(band, p, 2, 3, y_out).wait_recv()
        for slot, block in ((0, q), (1, q + 3), (2, q + 1), (3, q + 2)):
            for upper in range(2):
                owner = (block % BLOCKS + BLOCKS * upper) % depth
                view = returned.at[band, p, slot, :, pl.ds(upper * LANES, LANES)]
                target = mixed.at[z, pl.ds(band * band_rows, band_rows), pl.ds(p * LANES, LANES)]

                @pl.when(owner == z)
                def _():
                    target[...] = view[...]

                @pl.when(owner != z)
                def _():
                    remote(view, target, mixed_sem.at[0], mixed_sem.at[1], rank, owner).start()

    waiting = []
    bands_here, parts_here = set(), set()
    for until, band, p in ORDER:
        if until > step:
            weight_steps(step, until)
            step = until
        if band not in bands_here:
            bands_here.add(band)
            for slot in (1, 2, 3):
                view = gathered.at[band, :, slot]
                remote(view, view, rows_sem.at[0], rows_sem.at[3 * band + slot], x_up, z).wait_recv()
        if p not in parts_here:
            parts_here.add(p)
            half_part = weight.at[p, pl.ds(0, weight.shape[1] // 2)]
            remote(half_part, half_part, sent_sem.at[3], twin_sem.at[p], twin, z).wait_recv()
        project(band, p)
        waiting.append((band, p))
        if len(waiting) > LAG:
            deliver(*waiting.pop(0))
    for item in waiting:
        deliver(*item)

    edge_copy.wait_send()
    all_but_one(ends, ends_sem.at[0], ends_sem.at[1]).wait_send()
    all_but_one(back, back_sem.at[0], back_sem.at[1]).wait_send()

    def sent(view, sem):
        remote(view, view, sem, left_sem.at[0], x_up, z).wait_send()

    chain = weight.at[0, pl.ds(0, count * taken // 2)]
    sent(chain, sent_sem.at[0])

    @pl.when(down < BLOCKS - 1)
    def _():
        sent(chain, sent_sem.at[1])

    sent(weight.at[0, pl.ds(0, count * SHARED)], sent_sem.at[2])
    sent(weight.at[pl.ds(0, PARTS // 2)], sent_sem.at[3])
    sent(gathered.at[:, :, pl.ds(0, 3)], rows_sem.at[0])
    sent(leaving, return_sem.at[0])
    others = mixed.at[pl.ds(0, depth - 1)]
    remote(others, others, mixed_sem.at[0], mixed_sem.at[1], x_up, z).wait()


def on_device(projected, short_filter, bias, residue, rate, out_weight):
    ranks = lax.axis_size("seq")
    depth = lax.axis_size("grp")
    taken = projected[:, 0]
    rows, width = taken.shape[1:]
    modes = rate.shape[0]
    steps = rows // (GROUPS * BANDS)
    f32, bf16 = jnp.float32, jnp.bfloat16
    vmem = pl.BlockSpec(memory_space=pltpu.VMEM)
    exchanged = pltpu.VMEM((ranks, modes, width // ranks), f32)
    dma = pltpu.SemaphoreType.DMA
    return pl.pallas_call(
        functools.partial(block_kernel, ranks, steps, modes),
        in_specs=[pl.BlockSpec(memory_space=pl.ANY)] * 6,
        out_specs=vmem,
        out_shape=jax.ShapeDtypeStruct((depth, rows, out_weight.shape[1]), bf16),
        scratch_shapes=[
            pltpu.VMEM(taken.shape, bf16),
            pltpu.VMEM(short_filter.shape, f32),
            pltpu.VMEM(rate.shape, f32),
            pltpu.VMEM(residue.shape, f32),
            pltpu.VMEM((1, width), f32),
            pltpu.VMEM((3, 16, width), bf16),
            pltpu.VMEM((3, rows + 8, LANES), f32),
            pltpu.VMEM((steps * GROUPS, LANES), f32),
            pltpu.VMEM((BANDS * steps, GROUPS, width), f32),
            pltpu.VMEM((BANDS * steps, GROUPS, width), f32),
            pltpu.VMEM((BANDS, modes, GROUPS, width), f32),
            exchanged,
            pltpu.VMEM((8, width), f32),
            pltpu.VMEM((8, width), f32),
            exchanged,
            exchanged,
            exchanged,
            exchanged,
            pltpu.VMEM((PARTS, width, 2 * LANES), bf16),
            pltpu.VMEM((BANDS, ranks // SCOPE, BLOCKS, rows // BANDS, SCOPE * LANES), bf16),
            pltpu.VMEM((BLOCKS * rows // BANDS, 2 * LANES), f32),
            pltpu.VMEM((BANDS, PARTS, 3, rows // BANDS, 2 * LANES), bf16),
            pltpu.VMEM((BANDS, PARTS, BLOCKS, rows // BANDS, 2 * LANES), bf16),
            dma((2,)),
            dma((2,)),
            dma((1 + ranks // SCOPE,)),
            dma((PARTS * CHUNKS,)),
            dma((PARTS * CHUNKS,)),
            dma((PARTS * CHUNKS,)),
            dma((PARTS,)),
            dma((4,)),
            dma((1 + 3 * BANDS,)),
            dma((1 + 3 * BANDS * PARTS,)),
            dma((2,)),
            dma((5,)),
            dma((ranks // SCOPE,)),
        ],
        compiler_params=pltpu.CompilerParams(
            collective_id=0, has_side_effects=True, vmem_limit_bytes=62 * MIB
        ),
    )(taken, short_filter, rate, residue, bias[None], out_weight)


def solution(mesh):
    placed = (P(None, "grp", "seq", None), P(), P(), P(), P(), P(None, "grp"))
    return jax.shard_map(
        on_device, mesh=mesh, in_specs=placed, out_specs=P(None, "seq", "grp"), check_vma=False
    )
```
